32 devices in a mesh: blk: 8 (over y, x, core), head: 4 (over z).
Axes of the slice: x: 2, y: 2, z: 4, core: 2. Of those that a mesh axis runs over, the one named last changes fastest.
Arguments:
- hidden_in: bfloat16 [4096, 2048], P('blk'), may hold values from -6 to 6
- layer_input: bfloat16 [4096, 256], P(('blk', 'head')), may hold values from -6 to 6
- in_gain: float32 [2048], replicated, may hold values from 0.5 to 1.5
- w_query: bfloat16 [2048, 2048], P(None, 'head'), may hold values from -0.125 to 0.125
- w_keyval: bfloat16 [2048, 1024], P(None, 'head'), may hold values from -0.125 to 0.125
- q_gain: float32 [256], replicated, may hold values from 0.2 to 0.45
- k_gain: float32 [256], replicated, may hold values from 0.2 to 0.45
- w_out: bfloat16 [2048, 2048], P('head'), may hold values from -0.125 to 0.125
- post_gain: float32 [2048], replicated, may hold values from 0.5 to 1.5
- laurel_left: bfloat16 [2048, 64], replicated, may hold values from -0.125 to 0.125
- laurel_right: bfloat16 [64, 2048], replicated, may hold values from -0.75 to 0.75
- laurel_gain: float32 [2048], replicated, may hold values from 0.5 to 1.5
- w_plgate: bfloat16 [2048, 256], replicated, may hold values from -0.125 to 0.125
- w_plproj: bfloat16 [256, 2048], replicated, may hold values from -0.375 to 0.375
- pl_gain: float32 [2048], replicated, may hold values from 0.5 to 1.5
- kv_pool: bfloat16 [96, 4, 128, 256], P('blk'), may hold values from -44 to 44, as said below
- page_table: int32 [8, 12], P('blk'), may hold values from 0 to 11, each once within a row
- prefix_len: int32 [8], P('blk'), may hold values from 1 to 1536, as said below
- decode_owner: int32 [8], replicated, may hold values from 0 to 7, each once
Outputs:
- mixed: bfloat16 [4096, 2048], P(('blk', 'head'))
- decode_kv: bfloat16 [4, 8, 2048, 256], P('head', 'blk')
The draws below stay inside these ranges and needn't reach their ends.
Inputs may be any that keep to these rules, and one draw needn't show every extreme that they name: `kv_pool`: cached keys and values; one request's prefix fills its 12 pages in every draw. `page_table`: each row names each of its 12 pool pages once. `prefix_len`: some request has exactly 1536 cached tokens. `decode_owner`: each request has its own slot.
All inputs are finite; a program needn't handle non-finite values.
Results may differ from the reference program's by a relative error of at most 0.009.
Values may be sent and summed in bfloat16 or wider, within the bound.
A program may use at most 128 MiB of HBM per device.

```python
import math
import jax
import jax.numpy as jnp
from jax import lax

D = 2048
QH = 8
KVH = 2
HD = 256
RANK = 64
PLI = 256
NEW = 512
PAGE = 128
PAGES = 12
REQ = 8
TOKENS = 4096
POOL_PAGES = 96
N_HEAD = 4


def draw_kv_pool(key, part):
    key_normal = jax.random.fold_in(key, 0)
    pool_shape = (POOL_PAGES, 2 * KVH, PAGE, HD)
    values_raw = jnp.clip(jax.random.normal(key_normal, pool_shape, jnp.float32), -6.0, 6.0)
    is_key = (jnp.arange(2 * KVH) < KVH).reshape(1, 2 * KVH, 1, 1)
    factor = jnp.where(is_key, 0.3, 1.0)
    return (values_raw * factor).astype(jnp.bfloat16)


def draw_prefix_len(key, part):
    key_shift, key_cut, key_top = jax.random.split(key, 3)
    prefix_max = PAGES * PAGE
    shifts = jax.random.randint(key_shift, (REQ,), 0, 4)
    divisor = jnp.left_shift(jnp.ones((REQ,), jnp.int32), shifts)
    span_len = jnp.maximum(prefix_max // divisor, 1)
    cuts = jax.random.randint(key_cut, (REQ,), jnp.zeros((REQ,), jnp.int32), span_len)
    lengths = jnp.maximum(span_len - cuts, 1)
    chosen = jax.random.randint(key_top, (), 0, REQ)
    return jnp.where(jnp.arange(REQ) == chosen, prefix_max, lengths).astype(jnp.int32)


def level_of(key, dims, shards, low, top_value):
    level = 1.0
    for axis_at, shards_of in shards:
        draws = jax.random.uniform(jax.random.fold_in(jax.random.fold_in(key, 6), axis_at), (shards_of,), jnp.float32, low / len(shards), top_value / len(shards))
        level = level * jnp.repeat(jnp.exp(draws), dims[axis_at] // shards_of).reshape((-1,) + (1,) * (len(dims) - 1 - axis_at))
    return level


def centred(stream_key, extent, deviation, limit, cuts=(), kind=jnp.bfloat16):
    array = deviation * jax.random.normal(stream_key, extent, jnp.float32)
    if cuts:
        array = array * level_of(stream_key, extent, cuts, -0.22, 0.18)
    return jnp.clip(array, -limit, limit).astype(kind)


def setup_inputs(seed: int = 0) -> dict:
    keys = jax.random.split(jax.random.key(seed), 20)
    return {
        "hidden_in": centred(keys[0], (TOKENS, D), 1.0, 6.0, ((0, 8),)),
        "layer_input": centred(keys[1], (TOKENS, PLI), 1.0, 6.0, ((0, 32),)),
        "in_gain": jnp.clip(1.0 + 0.1 * jax.random.normal(keys[2], (D,), jnp.float32), 0.5, 1.5),
        "w_query": centred(keys[3], (D, QH * HD), D ** -0.5, 0.125, ((1, 4),)),
        "w_keyval": centred(keys[4], (D, 2 * KVH * HD), D ** -0.5, 0.125, ((1, 4),)),
        "q_gain": jnp.clip(jnp.exp(jax.random.uniform(keys[5], (HD,), jnp.float32, math.log(0.2), math.log(0.45))), 0.2, 0.45),
        "k_gain": jnp.clip(jnp.exp(jax.random.uniform(keys[6], (HD,), jnp.float32, math.log(0.2), math.log(0.45))), 0.2, 0.45),
        "w_out": centred(keys[7], (QH * HD, D), (QH * HD) ** -0.5, 0.125, ((0, 4),)),
        "post_gain": jnp.clip(1.0 + 0.1 * jax.random.normal(keys[8], (D,), jnp.float32), 0.5, 1.5),
        "laurel_left": centred(keys[9], (D, RANK), D ** -0.5, 0.125),
        "laurel_right": centred(keys[10], (RANK, D), RANK ** -0.5, 0.75),
        "laurel_gain": jnp.clip(1.0 + 0.1 * jax.random.normal(keys[11], (D,), jnp.float32), 0.5, 1.5),
        "w_plgate": centred(keys[12], (D, PLI), D ** -0.5, 0.125),
        "w_plproj": centred(keys[13], (PLI, D), PLI ** -0.5, 0.375),
        "pl_gain": jnp.clip(1.0 + 0.1 * jax.random.normal(keys[14], (D,), jnp.float32), 0.5, 1.5),
        "kv_pool": draw_kv_pool(jax.random.fold_in(keys[19], 71), 0),
        "page_table": jax.vmap(lambda own: jax.random.permutation(own, PAGES))(jax.random.split(keys[16], REQ)).reshape((REQ, PAGES)).astype(jnp.int32),
        "prefix_len": draw_prefix_len(jax.random.fold_in(keys[19], 71), 0),
        "decode_owner": jax.random.permutation(keys[18], REQ).astype(jnp.int32),
    }


eps = 1e-06
rope_base = 1000000.0

def rms_scale(values):
    return values * lax.rsqrt(lax.optimization_barrier(jnp.mean(values * values, axis=-1, keepdims=True)) + eps)

def rotate(values, positions):
    half_dim = values.shape[-1] // 2
    frequency = rope_base ** (-jnp.arange(half_dim, dtype=jnp.float32) / half_dim)
    angles = positions.astype(jnp.float32)[:, None] * frequency[None, :]
    cosine = jnp.cos(angles)
    sine_part = jnp.sin(angles)
    lower_half = values[..., :half_dim]
    upper_half = values[..., half_dim:]
    return jnp.concatenate([lower_half * cosine - upper_half * sine_part, upper_half * cosine + lower_half * sine_part], axis=-1)

def reference(hidden_in, layer_input, in_gain, w_query, w_keyval, q_gain, k_gain, w_out, post_gain, laurel_left, laurel_right, laurel_gain, w_plgate, w_plproj, pl_gain, kv_pool, page_table, prefix_len, decode_owner):
    prefix_max = PAGES * PAGE
    group_size = QH // KVH
    stretch_cols = QH * HD // N_HEAD

    def per_request(req_idx):
        tokens_in = lax.dynamic_slice_in_dim(hidden_in, req_idx * NEW, NEW, 0)
        plane_in = lax.dynamic_slice_in_dim(layer_input, req_idx * NEW, NEW, 0)
        length = prefix_len[req_idx]
        positions = length + jnp.arange(NEW, dtype=jnp.int32)
        normed = (rms_scale(tokens_in.astype(jnp.float32)) * in_gain).astype(jnp.bfloat16)
        queries = jnp.dot(normed, w_query, preferred_element_type=jnp.float32).reshape(NEW, QH, HD)
        queries = rotate(jnp.transpose(rms_scale(queries) * q_gain, (1, 0, 2)), positions).astype(jnp.bfloat16)
        kv_proj = rms_scale(jnp.dot(normed, w_keyval, preferred_element_type=jnp.float32).reshape(NEW, 2 * KVH, HD))
        kv_proj = jnp.transpose(kv_proj, (1, 0, 2))
        key_new = rotate(kv_proj[:KVH] * k_gain, positions)
        fresh = jnp.concatenate([key_new, kv_proj[KVH:]], axis=0).astype(jnp.bfloat16)
        pool_rows = lax.dynamic_slice_in_dim(kv_pool, req_idx * PAGES, PAGES, 0)
        table_row = page_table[req_idx]
        my_pages = jnp.take(pool_rows, table_row, axis=0)
        old_all = jnp.transpose(my_pages, (1, 0, 2, 3)).reshape(2 * KVH, prefix_max, HD)
        live_mask = jnp.arange(prefix_max, dtype=jnp.int32) < length
        old_all = jnp.where(live_mask[None, :, None], old_all, jnp.zeros_like(old_all))
        keys_all = jnp.concatenate([old_all[:KVH], fresh[:KVH]], axis=1).astype(jnp.float32)
        vals_all = jnp.concatenate([old_all[KVH:], fresh[KVH:]], axis=1).astype(jnp.float32)
        grouped_q = queries.reshape(KVH, group_size * NEW, HD).astype(jnp.float32)
        scores = jnp.einsum('gqd,gkd->gqk', grouped_q, keys_all)
        row_pos = jnp.tile(jnp.arange(NEW, dtype=jnp.int32), group_size)
        key_idx = jnp.arange(prefix_max + NEW, dtype=jnp.int32)
        allowed_old = (key_idx[None, :] < prefix_max) & (key_idx[None, :] < length)
        allowed_new = (key_idx[None, :] >= prefix_max) & (key_idx[None, :] - prefix_max <= row_pos[:, None])
        allowed = allowed_old | allowed_new
        scores = jnp.where(allowed[None], scores, -jnp.inf)
        row_top = lax.optimization_barrier(jnp.max(scores, axis=-1, keepdims=True))
        expo = jnp.exp(scores - row_top)
        row_total = lax.optimization_barrier(jnp.sum(expo, axis=-1, keepdims=True))
        weights = expo.astype(jnp.bfloat16)
        attn = jnp.einsum('gqk,gkd->gqd', weights.astype(jnp.float32), vals_all) / row_total
        attn = attn.astype(jnp.bfloat16).reshape(QH, NEW, HD)
        attn = jnp.transpose(attn, (1, 0, 2)).reshape(NEW, QH * HD)
        parts = jnp.einsum('tgc,gcd->gtd', attn.reshape(NEW, N_HEAD, stretch_cols).astype(jnp.float32), w_out.reshape(N_HEAD, stretch_cols, D).astype(jnp.float32))
        proj = lax.optimization_barrier(jnp.sum(parts.astype(jnp.bfloat16).astype(jnp.float32), axis=0))
        branch_low = jnp.dot(normed, laurel_left, preferred_element_type=jnp.float32).astype(jnp.bfloat16)
        laurel = normed.astype(jnp.float32) + rms_scale(jnp.dot(branch_low, laurel_right, preferred_element_type=jnp.float32)) * laurel_gain
        state = (tokens_in.astype(jnp.float32) + rms_scale(proj) * post_gain + laurel) * 2.0 ** (-0.5)
        state_b = state.astype(jnp.bfloat16)
        gated = (jax.nn.gelu(jnp.dot(state_b, w_plgate, preferred_element_type=jnp.float32), approximate=True) * plane_in.astype(jnp.float32)).astype(jnp.bfloat16)
        mixed_rows = (state + rms_scale(jnp.dot(gated, w_plproj, preferred_element_type=jnp.float32)) * pl_gain).astype(jnp.bfloat16)
        base_seq = jnp.concatenate([old_all, jnp.zeros((2 * KVH, NEW, HD), jnp.bfloat16)], axis=1)
        full_seq = lax.dynamic_update_slice(base_seq, fresh, (jnp.int32(0), length.astype(jnp.int32), jnp.int32(0)))
        return (mixed_rows, full_seq)
    mixed_all, seq_all = lax.map(per_request, jnp.arange(REQ, dtype=jnp.int32))
    mixed = mixed_all.reshape(REQ * NEW, D)
    inverse = jnp.zeros((REQ,), jnp.int32).at[decode_owner.astype(jnp.int32)].set(jnp.arange(REQ, dtype=jnp.int32))
    arranged = jnp.take(seq_all, inverse, axis=0)
    decode_kv = jnp.transpose(arranged, (1, 0, 2, 3))
    return (mixed, decode_kv)
```

```python
import functools

import jax
import jax.numpy as jnp
from jax import lax
from jax.experimental import pallas as pl
from jax.experimental.pallas import tpu as pltpu
from jax.sharding import PartitionSpec as P

QH = 8

eps = 1e-06
rope_base = 1000000.0
VMEM_BYTES = 40 * 1024 * 1024


def rms_scale(values):
    return values * lax.rsqrt(jnp.mean(values * values, axis=-1, keepdims=True) + eps)


def rotate(values, cosine, sine):
    half_dim = values.shape[-1] // 2
    lower = values[:, :half_dim]
    upper = values[:, half_dim:]
    return jnp.concatenate([lower * cosine - upper * sine, upper * cosine + lower * sine], axis=-1)


def matmul(rows, columns):
    return jnp.dot(rows, columns, preferred_element_type=jnp.float32)


def scores_of(rows, keys):
    return lax.dot_general(rows, keys, (((1,), (1,)), ((), ())), preferred_element_type=jnp.float32)


def call(body, out_shape, grid, in_specs, out_specs, scalars, operands, flops, moved, scratch=()):
    return pl.pallas_call(
        body,
        out_shape=out_shape,
        grid_spec=pltpu.PrefetchScalarGridSpec(
            num_scalar_prefetch=len(scalars),
            grid=grid,
            in_specs=in_specs,
            out_specs=out_specs,
            scratch_shapes=list(scratch),
        ),
        compiler_params=pltpu.CompilerParams(vmem_limit_bytes=VMEM_BYTES),
        cost_estimate=pl.CostEstimate(flops=flops, bytes_accessed=moved, transcendentals=0),
    )(*scalars, *operands)


def whole(shape):
    return pl.BlockSpec(shape, lambda *_: (0,) * len(shape))


def project_body(is_key, hidden, in_gain, w_query, w_keyval, q_gain, k_gain, cosine, sine, q_out, fresh_out):
    heads, _, head_dim = q_out.shape
    normed = (rms_scale(hidden[...].astype(jnp.float32)) * in_gain[...]).astype(jnp.bfloat16)
    cos, sin = cosine[...], sine[...]
    own = rms_scale(matmul(normed, w_keyval[...]))
    turned = rotate(own * k_gain[...], cos, sin)
    fresh_out[...] = jnp.where(is_key[0] > 0, turned, own).astype(jnp.bfloat16)
    queries = matmul(normed, w_query[...])
    for h in range(heads):
        part = queries[:, h * head_dim : (h + 1) * head_dim]
        q_out[h] = rotate(rms_scale(part) * q_gain[...], cos, sin).astype(jnp.bfloat16)


def sequence_body(table, place, fresh, pool, out, pages, wide, sems):
    n_pages = sems.shape[0]
    page_len = pool.shape[2]
    length = place[0]
    slot = place[1]
    copies = [
        pltpu.make_async_copy(
            pool.at[table[j], slot], pages.at[pl.ds(j * page_len, page_len)], sems.at[j]
        )
        for j in range(n_pages)
    ]
    for c in copies:
        c.start()
    prefix = n_pages * page_len
    rows = fresh.shape[0]
    wide[...] = jnp.zeros_like(wide)
    base = pl.multiple_of(lax.div(length, 8) * 8, 8)
    padded = jnp.concatenate([fresh[...].astype(jnp.float32), jnp.zeros((8, wide.shape[1]), jnp.float32)], axis=0)
    wide[pl.ds(base, rows + 8), :] = pltpu.roll(padded, lax.rem(length, 8), 0)
    for c in copies:
        c.wait()
    at = lax.broadcasted_iota(jnp.int32, (prefix, 1), 0)
    old = pages[...].astype(jnp.float32)
    out[:prefix, :] = jnp.where(at < length, old, wide[:prefix, :]).astype(jnp.bfloat16)
    out[prefix:, :] = wide[prefix : prefix + rows, :].astype(jnp.bfloat16)


def arrange_body(owner, spread, out, sems):
    n = spread.shape[0]

    def start(r, carry):
        pltpu.make_async_copy(spread.at[r], out.at[owner[r]], sems.at[r]).start()
        return carry

    def wait(r, carry):
        pltpu.make_async_copy(spread.at[r], out.at[owner[r]], sems.at[r]).wait()
        return carry

    lax.fori_loop(0, n, start, 0)
    lax.fori_loop(0, n, wait, 0)


def old_body(table, place, queries, pool, acc_out, top_out, total_out, keys, values, sems):
    n_pages = sems.shape[1]
    page_len = pool.shape[2]
    length = place[0]
    key_slot = place[1]
    value_slot = place[2]

    @pl.when(pl.program_id(0) == 0)
    def _():
        copies = []
        for j in range(n_pages):
            at = pl.ds(j * page_len, page_len)
            copies.append(pltpu.make_async_copy(pool.at[table[j], key_slot], keys.at[at], sems.at[0, j]))
        for j in range(n_pages):
            at = pl.ds(j * page_len, page_len)
            copies.append(pltpu.make_async_copy(pool.at[table[j], value_slot], values.at[at], sems.at[1, j]))
        for c in copies:
            c.start()
        for c in copies:
            c.wait()

    scores = scores_of(queries[...], keys[...])
    at = lax.broadcasted_iota(jnp.int32, (1, scores.shape[1]), 1)
    scores = jnp.where(at < length, scores, -jnp.inf)
    top = jnp.max(scores, axis=1, keepdims=True)
    expo = jnp.exp(scores - top)
    top_out[...] = top
    total_out[...] = jnp.sum(expo, axis=1, keepdims=True)
    acc_out[...] = matmul(expo.astype(jnp.bfloat16), values[...])


def new_body(place, queries, key, value, acc, top_in, total_in, w_out, part_out):
    heads, rows, head_dim = queries.shape
    new_rows = key.shape[1]
    row_at = lax.broadcasted_iota(jnp.int32, (rows, new_rows), 0) + pl.program_id(0) * rows
    causal = lax.broadcasted_iota(jnp.int32, (rows, new_rows), 1) <= row_at
    sides = []
    for h in range(heads):
        scores = jnp.where(causal, scores_of(queries[h], key[0]), -jnp.inf)
        top_old = top_in[h]
        top = jnp.maximum(top_old, jnp.max(scores, axis=1, keepdims=True))
        expo = jnp.exp(scores - top)
        scale = jnp.exp(top_old - top)
        total = total_in[h] * scale + jnp.sum(expo, axis=1, keepdims=True)
        mix = acc[h] * scale + matmul(expo.astype(jnp.bfloat16), value[0])
        sides.append((mix / total).astype(jnp.bfloat16))
    attn = jnp.concatenate(sides, axis=1)
    part_out[...] = matmul(attn, w_out[...]).astype(jnp.bfloat16)


def base_body(place, hidden, in_gain, left, right, laurel_gain, base_out):
    tokens = hidden[...].astype(jnp.float32)
    normed = (rms_scale(tokens) * in_gain[...]).astype(jnp.bfloat16)
    low = matmul(normed, left[...]).astype(jnp.bfloat16)
    laurel = normed.astype(jnp.float32) + rms_scale(matmul(low, right[...])) * laurel_gain[...]
    base_out[...] = tokens + laurel


def tail_body(base, proj, post_gain, layer_input, w_plgate, w_plproj, pl_gain, out):
    state = (base[...] + rms_scale(proj[...].astype(jnp.float32)) * post_gain[...]) * 2.0 ** (-0.5)
    gate = jax.nn.gelu(matmul(state.astype(jnp.bfloat16), w_plgate[...]), approximate=True)
    gated = (gate * layer_input[...].astype(jnp.float32)).astype(jnp.bfloat16)
    out[...] = (state + rms_scale(matmul(gated, w_plproj[...])) * pl_gain[...]).astype(jnp.bfloat16)


def on_device(
    hidden_in,
    layer_input,
    in_gain,
    w_query,
    w_keyval,
    q_gain,
    k_gain,
    w_out,
    post_gain,
    laurel_left,
    laurel_right,
    laurel_gain,
    w_plgate,
    w_plproj,
    pl_gain,
    kv_pool,
    page_table,
    prefix_len,
    decode_owner,
):
    new_rows, width = hidden_in.shape
    head_dim = kv_pool.shape[3]
    page_len = kv_pool.shape[2]
    n_pages = page_table.shape[1]
    kv_heads = kv_pool.shape[1] // 2
    local_heads = w_query.shape[1] // head_dim
    prefix_max = n_pages * page_len
    total_len = prefix_max + new_rows
    blocks = lax.axis_size("blk")
    block_span = total_len // blocks
    head_idx = lax.axis_index("head").astype(jnp.int32)
    kv_of = head_idx * local_heads // (QH // kv_heads)
    length = prefix_len[0]
    table = page_table[0]
    bf16, f32 = jnp.bfloat16, jnp.float32
    in_hbm = pl.BlockSpec(memory_space=pl.ANY)
    half_dim = head_dim // 2
    row = lambda v: v.reshape(1, -1)

    positions = length + jnp.arange(new_rows, dtype=jnp.int32)
    frequency = rope_base ** (-jnp.arange(half_dim, dtype=jnp.float32) / half_dim)
    angles = positions.astype(jnp.float32)[:, None] * frequency[None, :]
    cosine, sine = jnp.cos(angles), jnp.sin(angles)

    tile = new_rows // 2
    rows_of = lambda cols: pl.BlockSpec((tile, cols), lambda i, *_: (i, 0))
    queries, fresh = call(
        project_body,
        (
            jax.ShapeDtypeStruct((local_heads, new_rows, head_dim), bf16),
            jax.ShapeDtypeStruct((new_rows, head_dim), bf16),
        ),
        (new_rows // tile,),
        [
            rows_of(width),
            whole((1, width)),
            whole(w_query.shape),
            whole(w_keyval.shape),
            whole((1, head_dim)),
            whole((1, head_dim)),
            rows_of(half_dim),
            rows_of(half_dim),
        ],
        (
            pl.BlockSpec((local_heads, tile, head_dim), lambda i, *_: (0, i, 0)),
            rows_of(head_dim),
        ),
        [(head_idx < kv_heads).astype(jnp.int32).reshape(1)],
        [hidden_in, row(in_gain), w_query, w_keyval, row(q_gain), row(k_gain), cosine, sine],
        2 * new_rows * width * (local_heads + 1) * head_dim,
        8 << 20,
    )

    gathered = lax.all_gather(fresh[None], "head", axis=0, tiled=True)

    full_seq = call(
        sequence_body,
        jax.ShapeDtypeStruct((total_len, head_dim), bf16),
        (1,),
        [whole((new_rows, head_dim)), in_hbm],
        whole((total_len, head_dim)),
        [table, jnp.stack([length, head_idx])],
        [fresh, kv_pool],
        1 << 20,
        4 << 20,
        [
            pltpu.VMEM((prefix_max, head_dim), bf16),
            pltpu.VMEM((total_len + 8, head_dim), f32),
            pltpu.SemaphoreType.DMA((n_pages,)),
        ],
    )
    spread = lax.all_to_all(
        full_seq.reshape(blocks, block_span, head_dim), "blk", split_axis=0, concat_axis=0, tiled=True
    )

    place = jnp.stack([length, kv_of, kv_of + kv_heads])
    flat = local_heads * new_rows
    q_tile = flat // 4
    q_rows = lambda cols: pl.BlockSpec((q_tile, cols), lambda i, *_: (i, 0))
    acc, top, total = call(
        old_body,
        (
            jax.ShapeDtypeStruct((flat, head_dim), f32),
            jax.ShapeDtypeStruct((flat, 1), f32),
            jax.ShapeDtypeStruct((flat, 1), f32),
        ),
        (flat // q_tile,),
        [q_rows(head_dim), in_hbm],
        (q_rows(head_dim), q_rows(1), q_rows(1)),
        [table, place],
        [queries.reshape(flat, head_dim), kv_pool],
        8 * flat * prefix_max * head_dim,
        8 << 20,
        [
            pltpu.VMEM((prefix_max, head_dim), bf16),
            pltpu.VMEM((prefix_max, head_dim), bf16),
            pltpu.SemaphoreType.DMA((2, n_pages)),
        ],
    )

    heads_of = lambda cols: pl.BlockSpec((local_heads, tile, cols), lambda i, *_: (0, i, 0))
    part = call(
        new_body,
        jax.ShapeDtypeStruct((new_rows, width), bf16),
        (new_rows // tile,),
        [
            heads_of(head_dim),
            pl.BlockSpec((1, new_rows, head_dim), lambda i, p: (p[1], 0, 0)),
            pl.BlockSpec((1, new_rows, head_dim), lambda i, p: (p[2], 0, 0)),
            heads_of(head_dim),
            heads_of(1),
            heads_of(1),
            whole(w_out.shape),
        ],
        rows_of(width),
        [place],
        [
            queries,
            gathered,
            gathered,
            acc.reshape(local_heads, new_rows, head_dim),
            top.reshape(local_heads, new_rows, 1),
            total.reshape(local_heads, new_rows, 1),
            w_out,
        ],
        8 * flat * new_rows * head_dim,
        8 << 20,
    )
    proj_rows = lax.psum_scatter(part, "head", scatter_dimension=0, tiled=True)

    quarter = new_rows // lax.axis_size("head")
    rank = laurel_left.shape[1]
    gate_dim = w_plgate.shape[1]
    base = call(
        base_body,
        jax.ShapeDtypeStruct((quarter, width), f32),
        (1,),
        [
            pl.BlockSpec((quarter, width), lambda i, p: (p[0], 0)),
            whole((1, width)),
            whole((width, rank)),
            whole((rank, width)),
            whole((1, width)),
        ],
        whole((quarter, width)),
        [head_idx.reshape(1)],
        [hidden_in, row(in_gain), laurel_left, laurel_right, row(laurel_gain)],
        1 << 28,
        4 << 20,
    )

    arranged = call(
        arrange_body,
        jax.ShapeDtypeStruct(spread.shape, bf16),
        (1,),
        [in_hbm],
        in_hbm,
        [decode_owner],
        [spread],
        1 << 10,
        2 << 20,
        [pltpu.SemaphoreType.DMA((blocks,))],
    )
    owned = lax.all_to_all(arranged, "blk", split_axis=0, concat_axis=0, tiled=True)

    mixed = call(
        tail_body,
        jax.ShapeDtypeStruct((quarter, width), bf16),
        (1,),
        [
            whole((quarter, width)),
            whole((quarter, width)),
            whole((1, width)),
            whole((quarter, gate_dim)),
            whole(w_plgate.shape),
            whole(w_plproj.shape),
            whole((1, width)),
        ],
        whole((quarter, width)),
        [],
        [base, proj_rows, row(post_gain), layer_input, w_plgate, w_plproj, row(pl_gain)],
        1 << 28,
        6 << 20,
    )
    return (mixed, owned.reshape(1, 1, total_len, head_dim))


def solution(mesh):
    in_specs = (
        P("blk", None),
        P(("blk", "head"), None),
        P(),
        P(None, "head"),
        P(None, "head"),
        P(),
        P(),
        P("head", None),
        P(),
        P(),
        P(),
        P(),
        P(),
        P(),
        P(),
        P("blk", None, None, None),
        P("blk", None),
        P("blk"),
        P(),
    )
    out_specs = (P(("blk", "head"), None), P("head", "blk", None, None))
    return jax.shard_map(
        on_device, mesh=mesh, in_specs=in_specs, out_specs=out_specs, check_vma=False
    )
```

```python
import functools

import jax
import jax.numpy as jnp
from jax import lax
from jax.experimental import pallas as pl
from jax.experimental.pallas import tpu as pltpu
from jax.sharding import PartitionSpec as P

QH = 8

eps = 1e-06
rope_base = 1000000.0
VMEM_BYTES = 60 * 1024 * 1024


def rms_scale(values):
    return values * lax.rsqrt(jnp.mean(values * values, axis=-1, keepdims=True) + eps)


def rotate(values, cosine, sine):
    half_dim = values.shape[-1] // 2
    lower = values[:, :half_dim]
    upper = values[:, half_dim:]
    return jnp.concatenate([lower * cosine - upper * sine, upper * cosine + lower * sine], axis=-1)


def matmul(rows, columns):
    return jnp.dot(rows, columns, preferred_element_type=jnp.float32)


def scores_of(rows, keys):
    return lax.dot_general(rows, keys, (((1,), (1,)), ((), ())), preferred_element_type=jnp.float32)


def call(body, out_shape, grid, in_specs, out_specs, scalars, operands, flops, moved, scratch=()):
    return pl.pallas_call(
        body,
        out_shape=out_shape,
        grid_spec=pltpu.PrefetchScalarGridSpec(
            num_scalar_prefetch=len(scalars),
            grid=grid,
            in_specs=in_specs,
            out_specs=out_specs,
            scratch_shapes=list(scratch),
        ),
        compiler_params=pltpu.CompilerParams(vmem_limit_bytes=VMEM_BYTES),
        cost_estimate=pl.CostEstimate(flops=flops, bytes_accessed=moved, transcendentals=0),
    )(*scalars, *operands)


def whole(shape):
    return pl.BlockSpec(shape, lambda *_: (0,) * len(shape))


def project_body(is_key, hidden, in_gain, w_query, w_keyval, q_gain, k_gain, cosine, sine, q_out, fresh_out):
    heads, _, head_dim = q_out.shape
    normed = (rms_scale(hidden[...].astype(jnp.float32)) * in_gain[...]).astype(jnp.bfloat16)
    cos, sin = cosine[...], sine[...]
    own = rms_scale(matmul(normed, w_keyval[...]))
    turned = rotate(own * k_gain[...], cos, sin)
    fresh_out[...] = jnp.where(is_key[0] > 0, turned, own).astype(jnp.bfloat16)
    queries = matmul(normed, w_query[...])
    for h in range(heads):
        part = queries[:, h * head_dim : (h + 1) * head_dim]
        q_out[h] = rotate(rms_scale(part) * q_gain[...], cos, sin).astype(jnp.bfloat16)


def sequence_body(table, place, fresh, pool, out, pages, wide, sems):
    n_pages = sems.shape[0]
    page_len = pool.shape[2]
    length = place[0]
    slot = place[1]
    copies = [
        pltpu.make_async_copy(
            pool.at[table[j], slot], pages.at[pl.ds(j * page_len, page_len)], sems.at[j]
        )
        for j in range(n_pages)
    ]
    for c in copies:
        c.start()
    prefix = n_pages * page_len
    rows = fresh.shape[0]
    wide[...] = jnp.zeros_like(wide)
    base = pl.multiple_of(lax.div(length, 8) * 8, 8)
    padded = jnp.concatenate([fresh[...].astype(jnp.float32), jnp.zeros((8, wide.shape[1]), jnp.float32)], axis=0)
    wide[pl.ds(base, rows + 8), :] = pltpu.roll(padded, lax.rem(length, 8), 0)
    for c in copies:
        c.wait()
    at = lax.broadcasted_iota(jnp.int32, (prefix, 1), 0)
    old = pages[...].astype(jnp.float32)
    out[:prefix, :] = jnp.where(at < length, old, wide[:prefix, :]).astype(jnp.bfloat16)
    out[prefix:, :] = wide[prefix : prefix + rows, :].astype(jnp.bfloat16)


def arrange_body(owner, spread, out, sems):
    n = spread.shape[0]

    def start(r, carry):
        pltpu.make_async_copy(spread.at[r], out.at[owner[r]], sems.at[r]).start()
        return carry

    def wait(r, carry):
        pltpu.make_async_copy(spread.at[r], out.at[owner[r]], sems.at[r]).wait()
        return carry

    lax.fori_loop(0, n, start, 0)
    lax.fori_loop(0, n, wait, 0)


def old_body(table, place, queries, pool, acc_out, top_out, total_out, keys, values, sems):
    n_pages = sems.shape[1]
    page_len = pool.shape[2]
    length = place[0]
    key_slot = place[1]
    value_slot = place[2]

    @pl.when(pl.program_id(0) == 0)
    def _():
        copies = []
        for j in range(n_pages):
            at = pl.ds(j * page_len, page_len)
            copies.append(pltpu.make_async_copy(pool.at[table[j], key_slot], keys.at[at], sems.at[0, j]))
        for j in range(n_pages):
            at = pl.ds(j * page_len, page_len)
            copies.append(pltpu.make_async_copy(pool.at[table[j], value_slot], values.at[at], sems.at[1, j]))
        for c in copies:
            c.start()
        for c in copies:
            c.wait()

    scores = scores_of(queries[...], keys[...])
    at = lax.broadcasted_iota(jnp.int32, (1, scores.shape[1]), 1)
    scores = jnp.where(at < length, scores, -jnp.inf)
    top = jnp.max(scores, axis=1, keepdims=True)
    expo = jnp.exp(scores - top)
    top_out[...] = top
    total_out[...] = jnp.sum(expo, axis=1, keepdims=True)
    acc_out[...] = matmul(expo.astype(jnp.bfloat16), values[...])


def new_body(place, queries, own, first, second, acc, top_in, total_in, w_out, part_out, key, value):
    heads, rows, head_dim = queries.shape
    new_rows = own.shape[0]

    @pl.when(pl.program_id(0) == 0)
    def _():
        for at, source in enumerate((own, first, second)):
            for which, kept in enumerate((key, value)):

                @pl.when(place[which] == at)
                def _(source=source, kept=kept):
                    kept[...] = source[...]

    row_at = lax.broadcasted_iota(jnp.int32, (rows, new_rows), 0) + pl.program_id(0) * rows
    causal = lax.broadcasted_iota(jnp.int32, (rows, new_rows), 1) <= row_at
    sides = []
    for h in range(heads):
        scores = jnp.where(causal, scores_of(queries[h], key[...]), -jnp.inf)
        top_old = top_in[h]
        top = jnp.maximum(top_old, jnp.max(scores, axis=1, keepdims=True))
        expo = jnp.exp(scores - top)
        scale = jnp.exp(top_old - top)
        total = total_in[h] * scale + jnp.sum(expo, axis=1, keepdims=True)
        mix = acc[h] * scale + matmul(expo.astype(jnp.bfloat16), value[...])
        sides.append((mix / total).astype(jnp.bfloat16))
    attn = jnp.concatenate(sides, axis=1)
    part_out[...] = matmul(attn, w_out[...]).astype(jnp.bfloat16)


def base_body(place, hidden, in_gain, left, right, laurel_gain, base_out):
    tokens = hidden[...].astype(jnp.float32)
    normed = (rms_scale(tokens) * in_gain[...]).astype(jnp.bfloat16)
    low = matmul(normed, left[...]).astype(jnp.bfloat16)
    laurel = normed.astype(jnp.float32) + rms_scale(matmul(low, right[...])) * laurel_gain[...]
    base_out[...] = tokens + laurel


def tail_body(base, proj, post_gain, layer_input, w_plgate, w_plproj, pl_gain, out):
    state = (base[...] + rms_scale(proj[...].astype(jnp.float32)) * post_gain[...]) * 2.0 ** (-0.5)
    gate = jax.nn.gelu(matmul(state.astype(jnp.bfloat16), w_plgate[...]), approximate=True)
    gated = (gate * layer_input[...].astype(jnp.float32)).astype(jnp.bfloat16)
    out[...] = (state + rms_scale(matmul(gated, w_plproj[...])) * pl_gain[...]).astype(jnp.bfloat16)


def on_device(
    hidden_in,
    layer_input,
    in_gain,
    w_query,
    w_keyval,
    q_gain,
    k_gain,
    w_out,
    post_gain,
    laurel_left,
    laurel_right,
    laurel_gain,
    w_plgate,
    w_plproj,
    pl_gain,
    kv_pool,
    page_table,
    prefix_len,
    decode_owner,
):
    new_rows, width = hidden_in.shape
    head_dim = kv_pool.shape[3]
    page_len = kv_pool.shape[2]
    n_pages = page_table.shape[1]
    kv_heads = kv_pool.shape[1] // 2
    local_heads = w_query.shape[1] // head_dim
    prefix_max = n_pages * page_len
    total_len = prefix_max + new_rows
    blocks = lax.axis_size("blk")
    block_span = total_len // blocks
    head_idx = lax.axis_index("head").astype(jnp.int32)
    kv_of = head_idx * local_heads // (QH // kv_heads)
    length = prefix_len[0]
    table = page_table[0]
    bf16, f32 = jnp.bfloat16, jnp.float32
    in_hbm = pl.BlockSpec(memory_space=pl.ANY)
    half_dim = head_dim // 2
    row = lambda v: v.reshape(1, -1)

    positions = length + jnp.arange(new_rows, dtype=jnp.int32)
    frequency = rope_base ** (-jnp.arange(half_dim, dtype=jnp.float32) / half_dim)
    angles = positions.astype(jnp.float32)[:, None] * frequency[None, :]
    cosine, sine = jnp.cos(angles), jnp.sin(angles)

    tile = new_rows // 2
    rows_of = lambda cols: pl.BlockSpec((tile, cols), lambda i, *_: (i, 0))
    queries, fresh = call(
        project_body,
        (
            jax.ShapeDtypeStruct((local_heads, new_rows, head_dim), bf16),
            jax.ShapeDtypeStruct((new_rows, head_dim), bf16),
        ),
        (new_rows // tile,),
        [
            rows_of(width),
            whole((1, width)),
            whole(w_query.shape),
            whole(w_keyval.shape),
            whole((1, head_dim)),
            whole((1, head_dim)),
            rows_of(half_dim),
            rows_of(half_dim),
        ],
        (
            pl.BlockSpec((local_heads, tile, head_dim), lambda i, *_: (0, i, 0)),
            rows_of(head_dim),
        ),
        [(head_idx < kv_heads).astype(jnp.int32).reshape(1)],
        [hidden_in, row(in_gain), w_query, w_keyval, row(q_gain), row(k_gain), cosine, sine],
        2 * new_rows * width * (local_heads + 1) * head_dim,
        8 << 20,
    )

    first = lax.ppermute(fresh, "head", [(0, 1), (1, 2), (2, 0)])
    second = lax.ppermute(fresh, "head", [(1, 3), (2, 1), (3, 2)])
    key_from = jnp.where(head_idx == 0, 0, jnp.where(head_idx == 3, 2, 1))
    value_from = jnp.where(head_idx == 0, 1, jnp.where(head_idx == 3, 0, 2))

    full_seq = call(
        sequence_body,
        jax.ShapeDtypeStruct((total_len, head_dim), bf16),
        (1,),
        [whole((new_rows, head_dim)), in_hbm],
        whole((total_len, head_dim)),
        [table, jnp.stack([length, head_idx])],
        [fresh, kv_pool],
        1 << 20,
        4 << 20,
        [
            pltpu.VMEM((prefix_max, head_dim), bf16),
            pltpu.VMEM((total_len + 8, head_dim), f32),
            pltpu.SemaphoreType.DMA((n_pages,)),
        ],
    )
    place = jnp.stack([length, kv_of, kv_of + kv_heads])
    flat = local_heads * new_rows
    queries, full_seq = lax.optimization_barrier((queries, full_seq))
    spread = lax.all_to_all(
        full_seq.reshape(blocks, block_span, head_dim), "blk", split_axis=0, concat_axis=0, tiled=True
    )
    q_tile = flat // 4
    q_rows = lambda cols: pl.BlockSpec((q_tile, cols), lambda i, *_: (i, 0))
    acc, top, total = call(
        old_body,
        (
            jax.ShapeDtypeStruct((flat, head_dim), f32),
            jax.ShapeDtypeStruct((flat, 1), f32),
            jax.ShapeDtypeStruct((flat, 1), f32),
        ),
        (flat // q_tile,),
        [q_rows(head_dim), in_hbm],
        (q_rows(head_dim), q_rows(1), q_rows(1)),
        [table, place],
        [queries.reshape(flat, head_dim), kv_pool],
        10 << 30,
        8 << 20,
        [
            pltpu.VMEM((prefix_max, head_dim), bf16),
            pltpu.VMEM((prefix_max, head_dim), bf16),
            pltpu.SemaphoreType.DMA((2, n_pages)),
        ],
    )

    heads_of = lambda cols: pl.BlockSpec((local_heads, tile, cols), lambda i, *_: (0, i, 0))
    part = call(
        new_body,
        jax.ShapeDtypeStruct((new_rows, width), bf16),
        (new_rows // tile,),
        [
            heads_of(head_dim),
            whole((new_rows, head_dim)),
            whole((new_rows, head_dim)),
            whole((new_rows, head_dim)),
            heads_of(head_dim),
            heads_of(1),
            heads_of(1),
            whole(w_out.shape),
        ],
        rows_of(width),
        [jnp.stack([key_from, value_from]).astype(jnp.int32)],
        [
            queries,
            fresh,
            first,
            second,
            acc.reshape(local_heads, new_rows, head_dim),
            top.reshape(local_heads, new_rows, 1),
            total.reshape(local_heads, new_rows, 1),
            w_out,
        ],
        6 << 30,
        8 << 20,
        [pltpu.VMEM((new_rows, head_dim), bf16), pltpu.VMEM((new_rows, head_dim), bf16)],
    )
    part, spread = lax.optimization_barrier((part, spread))
    proj_rows = lax.psum_scatter(part, "head", scatter_dimension=0, tiled=True)

    quarter = new_rows // lax.axis_size("head")
    rank = laurel_left.shape[1]
    gate_dim = w_plgate.shape[1]
    base = call(
        base_body,
        jax.ShapeDtypeStruct((quarter, width), f32),
        (1,),
        [
            pl.BlockSpec((quarter, width), lambda i, p: (p[0], 0)),
            whole((1, width)),
            whole((width, rank)),
            whole((rank, width)),
            whole((1, width)),
        ],
        whole((quarter, width)),
        [head_idx.reshape(1)],
        [hidden_in, row(in_gain), laurel_left, laurel_right, row(laurel_gain)],
        1 << 28,
        4 << 20,
    )

    arranged = call(
        arrange_body,
        jax.ShapeDtypeStruct(spread.shape, bf16),
        (1,),
        [in_hbm],
        in_hbm,
        [decode_owner],
        [spread],
        1 << 10,
        2 << 20,
        [pltpu.SemaphoreType.DMA((blocks,))],
    )
    owned = lax.all_to_all(arranged, "blk", split_axis=0, concat_axis=0, tiled=True)

    mixed = call(
        tail_body,
        jax.ShapeDtypeStruct((quarter, width), bf16),
        (1,),
        [
            whole((quarter, width)),
            whole((quarter, width)),
            whole((1, width)),
            whole((quarter, gate_dim)),
            whole(w_plgate.shape),
            whole(w_plproj.shape),
            whole((1, width)),
        ],
        whole((quarter, width)),
        [],
        [base, proj_rows, row(post_gain), layer_input, w_plgate, w_plproj, row(pl_gain)],
        1 << 28,
        6 << 20,
    )
    return (mixed, owned.reshape(1, 1, total_len, head_dim))


def solution(mesh):
    in_specs = (
        P("blk", None),
        P(("blk", "head"), None),
        P(),
        P(None, "head"),
        P(None, "head"),
        P(),
        P(),
        P("head", None),
        P(),
        P(),
        P(),
        P(),
        P(),
        P(),
        P(),
        P("blk", None, None, None),
        P("blk", None),
        P("blk"),
        P(),
    )
    out_specs = (P(("blk", "head"), None), P("head", "blk", None, None))
    return jax.shard_map(
        on_device, mesh=mesh, in_specs=in_specs, out_specs=out_specs, check_vma=False
    )
```

```python
import functools

import jax
import jax.numpy as jnp
from jax import lax
from jax.experimental import pallas as pl
from jax.experimental.pallas import tpu as pltpu
from jax.sharding import PartitionSpec as P

QH = 8

eps = 1e-06
rope_base = 1000000.0
VMEM_BYTES = 60 * 1024 * 1024


def rms_scale(values):
    return values * lax.rsqrt(jnp.mean(values * values, axis=-1, keepdims=True) + eps)


def rotate(values, cosine, sine):
    half_dim = values.shape[-1] // 2
    lower = values[:, :half_dim]
    upper = values[:, half_dim:]
    return jnp.concatenate([lower * cosine - upper * sine, upper * cosine + lower * sine], axis=-1)


def matmul(rows, columns):
    return jnp.dot(rows, columns, preferred_element_type=jnp.float32)


def scores_of(rows, keys):
    return lax.dot_general(rows, keys, (((1,), (1,)), ((), ())), preferred_element_type=jnp.float32)


def call(body, out_shape, grid, in_specs, out_specs, scalars, operands, flops, moved, scratch=()):
    return pl.pallas_call(
        body,
        out_shape=out_shape,
        grid_spec=pltpu.PrefetchScalarGridSpec(
            num_scalar_prefetch=len(scalars),
            grid=grid,
            in_specs=in_specs,
            out_specs=out_specs,
            scratch_shapes=list(scratch),
        ),
        compiler_params=pltpu.CompilerParams(vmem_limit_bytes=VMEM_BYTES),
        cost_estimate=pl.CostEstimate(flops=flops, bytes_accessed=moved, transcendentals=0),
    )(*scalars, *operands)


def whole(shape):
    return pl.BlockSpec(shape, lambda *_: (0,) * len(shape))


def project_body(is_key, hidden, in_gain, w_query, w_keyval, q_gain, k_gain, cosine, sine, q_out, fresh_out):
    heads, _, head_dim = q_out.shape
    normed = (rms_scale(hidden[...].astype(jnp.float32)) * in_gain[...]).astype(jnp.bfloat16)
    cos, sin = cosine[...], sine[...]
    own = rms_scale(matmul(normed, w_keyval[...]))
    turned = rotate(own * k_gain[...], cos, sin)
    fresh_out[...] = jnp.where(is_key[0] > 0, turned, own).astype(jnp.bfloat16)
    queries = matmul(normed, w_query[...])
    for h in range(heads):
        part = queries[:, h * head_dim : (h + 1) * head_dim]
        q_out[h] = rotate(rms_scale(part) * q_gain[...], cos, sin).astype(jnp.bfloat16)


def sequence_body(table, place, fresh, pool, out, pages, wide, sems):
    n_pages = sems.shape[0]
    page_len = pool.shape[2]
    length = place[0]
    slot = place[1]
    copies = [
        pltpu.make_async_copy(
            pool.at[table[j], slot], pages.at[pl.ds(j * page_len, page_len)], sems.at[j]
        )
        for j in range(n_pages)
    ]
    for c in copies:
        c.start()
    prefix = n_pages * page_len
    rows = fresh.shape[0]
    wide[...] = jnp.zeros_like(wide)
    base = pl.multiple_of(lax.div(length, 8) * 8, 8)
    padded = jnp.concatenate([fresh[...].astype(jnp.float32), jnp.zeros((8, wide.shape[1]), jnp.float32)], axis=0)
    wide[pl.ds(base, rows + 8), :] = pltpu.roll(padded, lax.rem(length, 8), 0)
    for c in copies:
        c.wait()
    at = lax.broadcasted_iota(jnp.int32, (prefix, 1), 0)
    old = pages[...].astype(jnp.float32)
    out[:prefix, :] = jnp.where(at < length, old, wide[:prefix, :]).astype(jnp.bfloat16)
    out[prefix:, :] = wide[prefix : prefix + rows, :].astype(jnp.bfloat16)


def arrange_body(owner, spread, out):
    def move(r, carry):
        out[owner[r]] = spread[r]
        return carry

    lax.fori_loop(0, spread.shape[0], move, 0)


def old_body(table, place, queries, pool, acc_out, top_out, total_out, keys, values, sems):
    n_pages = sems.shape[1]
    page_len = pool.shape[2]
    length = place[0]
    key_slot = place[1]
    value_slot = place[2]

    @pl.when(pl.program_id(0) == 0)
    def _():
        copies = []
        for j in range(n_pages):
            at = pl.ds(j * page_len, page_len)
            copies.append(pltpu.make_async_copy(pool.at[table[j], key_slot], keys.at[at], sems.at[0, j]))
        for j in range(n_pages):
            at = pl.ds(j * page_len, page_len)
            copies.append(pltpu.make_async_copy(pool.at[table[j], value_slot], values.at[at], sems.at[1, j]))
        for c in copies:
            c.start()
        for c in copies:
            c.wait()

    scores = scores_of(queries[...], keys[...])
    at = lax.broadcasted_iota(jnp.int32, (1, scores.shape[1]), 1)
    scores = jnp.where(at < length, scores, -jnp.inf)
    top = jnp.max(scores, axis=1, keepdims=True)
    expo = jnp.exp(scores - top)
    top_out[...] = top
    total_out[...] = jnp.sum(expo, axis=1, keepdims=True)
    acc_out[...] = matmul(expo.astype(jnp.bfloat16), values[...])


def new_body(place, queries, own, first, second, acc, top_in, total_in, w_out, part_out, key, value):
    heads, rows, head_dim = queries.shape
    new_rows = own.shape[0]

    @pl.when(pl.program_id(0) == 0)
    def _():
        for at, source in enumerate((own, first, second)):
            for which, kept in enumerate((key, value)):

                @pl.when(place[which] == at)
                def _(source=source, kept=kept):
                    kept[...] = source[...]

    row_at = lax.broadcasted_iota(jnp.int32, (rows, new_rows), 0) + pl.program_id(0) * rows
    causal = lax.broadcasted_iota(jnp.int32, (rows, new_rows), 1) <= row_at
    sides = []
    for h in range(heads):
        scores = jnp.where(causal, scores_of(queries[h], key[...]), -jnp.inf)
        top_old = top_in[h]
        top = jnp.maximum(top_old, jnp.max(scores, axis=1, keepdims=True))
        expo = jnp.exp(scores - top)
        scale = jnp.exp(top_old - top)
        total = total_in[h] * scale + jnp.sum(expo, axis=1, keepdims=True)
        mix = acc[h] * scale + matmul(expo.astype(jnp.bfloat16), value[...])
        sides.append((mix / total).astype(jnp.bfloat16))
    attn = jnp.concatenate(sides, axis=1)
    part_out[...] = matmul(attn, w_out[...]).astype(jnp.bfloat16)


def base_body(place, hidden, in_gain, left, right, laurel_gain, base_out):
    tokens = hidden[...].astype(jnp.float32)
    normed = (rms_scale(tokens) * in_gain[...]).astype(jnp.bfloat16)
    low = matmul(normed, left[...]).astype(jnp.bfloat16)
    laurel = normed.astype(jnp.float32) + rms_scale(matmul(low, right[...])) * laurel_gain[...]
    base_out[...] = tokens + laurel


def tail_body(base, proj, post_gain, layer_input, w_plgate, w_plproj, pl_gain, out):
    state = (base[...] + rms_scale(proj[...].astype(jnp.float32)) * post_gain[...]) * 2.0 ** (-0.5)
    gate = jax.nn.gelu(matmul(state.astype(jnp.bfloat16), w_plgate[...]), approximate=True)
    gated = (gate * layer_input[...].astype(jnp.float32)).astype(jnp.bfloat16)
    out[...] = (state + rms_scale(matmul(gated, w_plproj[...])) * pl_gain[...]).astype(jnp.bfloat16)


def on_device(
    hidden_in,
    layer_input,
    in_gain,
    w_query,
    w_keyval,
    q_gain,
    k_gain,
    w_out,
    post_gain,
    laurel_left,
    laurel_right,
    laurel_gain,
    w_plgate,
    w_plproj,
    pl_gain,
    kv_pool,
    page_table,
    prefix_len,
    decode_owner,
):
    new_rows, width = hidden_in.shape
    head_dim = kv_pool.shape[3]
    page_len = kv_pool.shape[2]
    n_pages = page_table.shape[1]
    kv_heads = kv_pool.shape[1] // 2
    local_heads = w_query.shape[1] // head_dim
    prefix_max = n_pages * page_len
    total_len = prefix_max + new_rows
    blocks = lax.axis_size("blk")
    block_span = total_len // blocks
    head_idx = lax.axis_index("head").astype(jnp.int32)
    kv_of = head_idx * local_heads // (QH // kv_heads)
    length = prefix_len[0]
    table = page_table[0]
    bf16, f32 = jnp.bfloat16, jnp.float32
    in_hbm = pl.BlockSpec(memory_space=pl.ANY)
    half_dim = head_dim // 2
    row = lambda v: v.reshape(1, -1)

    positions = length + jnp.arange(new_rows, dtype=jnp.int32)
    frequency = rope_base ** (-jnp.arange(half_dim, dtype=jnp.float32) / half_dim)
    angles = positions.astype(jnp.float32)[:, None] * frequency[None, :]
    cosine, sine = jnp.cos(angles), jnp.sin(angles)

    tile = new_rows // 2
    rows_of = lambda cols: pl.BlockSpec((tile, cols), lambda i, *_: (i, 0))
    queries, fresh = call(
        project_body,
        (
            jax.ShapeDtypeStruct((local_heads, new_rows, head_dim), bf16),
            jax.ShapeDtypeStruct((new_rows, head_dim), bf16),
        ),
        (new_rows // tile,),
        [
            rows_of(width),
            whole((1, width)),
            whole(w_query.shape),
            whole(w_keyval.shape),
            whole((1, head_dim)),
            whole((1, head_dim)),
            rows_of(half_dim),
            rows_of(half_dim),
        ],
        (
            pl.BlockSpec((local_heads, tile, head_dim), lambda i, *_: (0, i, 0)),
            rows_of(head_dim),
        ),
        [(head_idx < kv_heads).astype(jnp.int32).reshape(1)],
        [hidden_in, row(in_gain), w_query, w_keyval, row(q_gain), row(k_gain), cosine, sine],
        2 * new_rows * width * (local_heads + 1) * head_dim,
        8 << 20,
    )

    first = lax.ppermute(fresh, "head", [(0, 1), (1, 2), (2, 0)])
    second = lax.ppermute(fresh, "head", [(1, 3), (2, 1), (3, 2)])
    key_from = jnp.where(head_idx == 0, 0, jnp.where(head_idx == 3, 2, 1))
    value_from = jnp.where(head_idx == 0, 1, jnp.where(head_idx == 3, 0, 2))

    full_seq = call(
        sequence_body,
        jax.ShapeDtypeStruct((total_len, head_dim), bf16),
        (1,),
        [whole((new_rows, head_dim)), in_hbm],
        whole((total_len, head_dim)),
        [table, jnp.stack([length, head_idx])],
        [fresh, kv_pool],
        1 << 20,
        4 << 20,
        [
            pltpu.VMEM((prefix_max, head_dim), bf16),
            pltpu.VMEM((total_len + 8, head_dim), f32),
            pltpu.SemaphoreType.DMA((n_pages,)),
        ],
    )
    place = jnp.stack([length, kv_of, kv_of + kv_heads])
    flat = local_heads * new_rows
    queries, full_seq = lax.optimization_barrier((queries, full_seq))
    spread = lax.all_to_all(
        full_seq.reshape(blocks, block_span, head_dim), "blk", split_axis=0, concat_axis=0, tiled=True
    )
    q_tile = flat // 4
    q_rows = lambda cols: pl.BlockSpec((q_tile, cols), lambda i, *_: (i, 0))
    acc, top, total = call(
        old_body,
        (
            jax.ShapeDtypeStruct((flat, head_dim), f32),
            jax.ShapeDtypeStruct((flat, 1), f32),
            jax.ShapeDtypeStruct((flat, 1), f32),
        ),
        (flat // q_tile,),
        [q_rows(head_dim), in_hbm],
        (q_rows(head_dim), q_rows(1), q_rows(1)),
        [table, place],
        [queries.reshape(flat, head_dim), kv_pool],
        10 << 30,
        8 << 20,
        [
            pltpu.VMEM((prefix_max, head_dim), bf16),
            pltpu.VMEM((prefix_max, head_dim), bf16),
            pltpu.SemaphoreType.DMA((2, n_pages)),
        ],
    )

    heads_of = lambda cols: pl.BlockSpec((local_heads, tile, cols), lambda i, *_: (0, i, 0))
    part = call(
        new_body,
        jax.ShapeDtypeStruct((new_rows, width), bf16),
        (new_rows // tile,),
        [
            heads_of(head_dim),
            whole((new_rows, head_dim)),
            whole((new_rows, head_dim)),
            whole((new_rows, head_dim)),
            heads_of(head_dim),
            heads_of(1),
            heads_of(1),
            whole(w_out.shape),
        ],
        rows_of(width),
        [jnp.stack([key_from, value_from]).astype(jnp.int32)],
        [
            queries,
            fresh,
            first,
            second,
            acc.reshape(local_heads, new_rows, head_dim),
            top.reshape(local_heads, new_rows, 1),
            total.reshape(local_heads, new_rows, 1),
            w_out,
        ],
        6 << 30,
        8 << 20,
        [pltpu.VMEM((new_rows, head_dim), bf16), pltpu.VMEM((new_rows, head_dim), bf16)],
    )
    part, spread = lax.optimization_barrier((part, spread))
    proj_rows = lax.psum_scatter(part, "head", scatter_dimension=0, tiled=True)

    quarter = new_rows // lax.axis_size("head")
    rank = laurel_left.shape[1]
    gate_dim = w_plgate.shape[1]
    base = call(
        base_body,
        jax.ShapeDtypeStruct((quarter, width), f32),
        (1,),
        [
            pl.BlockSpec((quarter, width), lambda i, p: (p[0], 0)),
            whole((1, width)),
            whole((width, rank)),
            whole((rank, width)),
            whole((1, width)),
        ],
        whole((quarter, width)),
        [head_idx.reshape(1)],
        [hidden_in, row(in_gain), laurel_left, laurel_right, row(laurel_gain)],
        1 << 28,
        4 << 20,
    )

    arranged = call(
        arrange_body,
        jax.ShapeDtypeStruct(spread.shape, bf16),
        (1,),
        [whole(spread.shape)],
        whole(spread.shape),
        [decode_owner],
        [spread],
        1 << 10,
        2 << 20,
    )
    owned = lax.all_to_all(arranged, "blk", split_axis=0, concat_axis=0, tiled=True)

    mixed = call(
        tail_body,
        jax.ShapeDtypeStruct((quarter, width), bf16),
        (1,),
        [
            whole((quarter, width)),
            whole((quarter, width)),
            whole((1, width)),
            whole((quarter, gate_dim)),
            whole(w_plgate.shape),
            whole(w_plproj.shape),
            whole((1, width)),
        ],
        whole((quarter, width)),
        [],
        [base, proj_rows, row(post_gain), layer_input, w_plgate, w_plproj, row(pl_gain)],
        1 << 28,
        6 << 20,
    )
    return (mixed, owned.reshape(1, 1, total_len, head_dim))


def solution(mesh):
    in_specs = (
        P("blk", None),
        P(("blk", "head"), None),
        P(),
        P(None, "head"),
        P(None, "head"),
        P(),
        P(),
        P("head", None),
        P(),
        P(),
        P(),
        P(),
        P(),
        P(),
        P(),
        P("blk", None, None, None),
        P("blk", None),
        P("blk"),
        P(),
    )
    out_specs = (P(("blk", "head"), None), P("head", "blk", None, None))
    return jax.shard_map(
        on_device, mesh=mesh, in_specs=in_specs, out_specs=out_specs, check_vma=False
    )
```

```python
import functools

import jax
import jax.numpy as jnp
from jax import lax
from jax.experimental import pallas as pl
from jax.experimental.pallas import tpu as pltpu
from jax.sharding import PartitionSpec as P

QH = 8

eps = 1e-06
rope_base = 1000000.0
VMEM_BYTES = 60 * 1024 * 1024


def rms_scale(values):
    return values * lax.rsqrt(jnp.mean(values * values, axis=-1, keepdims=True) + eps)


def rotate(values, cosine, sine):
    half_dim = values.shape[-1] // 2
    lower = values[:, :half_dim]
    upper = values[:, half_dim:]
    return jnp.concatenate([lower * cosine - upper * sine, upper * cosine + lower * sine], axis=-1)


def matmul(rows, columns):
    return jnp.dot(rows, columns, preferred_element_type=jnp.float32)


def scores_of(rows, keys):
    return lax.dot_general(rows, keys, (((1,), (1,)), ((), ())), preferred_element_type=jnp.float32)


def call(body, out_shape, grid, in_specs, out_specs, scalars, operands, flops, moved, scratch=()):
    return pl.pallas_call(
        body,
        out_shape=out_shape,
        grid_spec=pltpu.PrefetchScalarGridSpec(
            num_scalar_prefetch=len(scalars),
            grid=grid,
            in_specs=in_specs,
            out_specs=out_specs,
            scratch_shapes=list(scratch),
        ),
        compiler_params=pltpu.CompilerParams(vmem_limit_bytes=VMEM_BYTES),
        cost_estimate=pl.CostEstimate(flops=flops, bytes_accessed=moved, transcendentals=0),
    )(*scalars, *operands)


def whole(shape):
    return pl.BlockSpec(shape, lambda *_: (0,) * len(shape))


def project_body(is_key, hidden, in_gain, w_query, w_keyval, q_gain, k_gain, cosine, sine, q_out, fresh_out):
    heads, _, head_dim = q_out.shape
    normed = (rms_scale(hidden[...].astype(jnp.float32)) * in_gain[...]).astype(jnp.bfloat16)
    cos, sin = cosine[...], sine[...]
    own = rms_scale(matmul(normed, w_keyval[...]))
    turned = rotate(own * k_gain[...], cos, sin)
    fresh_out[...] = jnp.where(is_key[0] > 0, turned, own).astype(jnp.bfloat16)
    queries = matmul(normed, w_query[...])
    for h in range(heads):
        part = queries[:, h * head_dim : (h + 1) * head_dim]
        q_out[h] = rotate(rms_scale(part) * q_gain[...], cos, sin).astype(jnp.bfloat16)


def sequence_body(table, place, fresh, pool, out, pages, wide, sems):
    n_pages = sems.shape[0]
    page_len = pool.shape[2]
    length = place[0]
    slot = place[1]
    copies = [
        pltpu.make_async_copy(
            pool.at[table[j], slot], pages.at[pl.ds(j * page_len, page_len)], sems.at[j]
        )
        for j in range(n_pages)
    ]
    for c in copies:
        c.start()
    prefix = n_pages * page_len
    rows = fresh.shape[0]
    wide[...] = jnp.zeros_like(wide)
    base = pl.multiple_of(lax.div(length, 8) * 8, 8)
    padded = jnp.concatenate([fresh[...].astype(jnp.float32), jnp.zeros((8, wide.shape[1]), jnp.float32)], axis=0)
    wide[pl.ds(base, rows + 8), :] = pltpu.roll(padded, lax.rem(length, 8), 0)
    for c in copies:
        c.wait()
    at = lax.broadcasted_iota(jnp.int32, (prefix, 1), 0)
    old = pages[...].astype(jnp.float32)
    out[:prefix, :] = jnp.where(at < length, old, wide[:prefix, :]).astype(jnp.bfloat16)
    out[prefix:, :] = wide[prefix : prefix + rows, :].astype(jnp.bfloat16)


def arrange_body(owner, spread, out):
    def move(r, carry):
        out[owner[r]] = spread[r]
        return carry

    lax.fori_loop(0, spread.shape[0], move, 0)


def old_body(table, place, queries, pool, acc_out, top_out, total_out, keys, values, sems):
    n_pages = sems.shape[1]
    page_len = pool.shape[2]
    length = place[0]
    key_slot = place[1]
    value_slot = place[2]

    @pl.when(pl.program_id(0) == 0)
    def _():
        copies = []
        for j in range(n_pages):
            at = pl.ds(j * page_len, page_len)
            copies.append(pltpu.make_async_copy(pool.at[table[j], key_slot], keys.at[at], sems.at[0, j]))
        for j in range(n_pages):
            at = pl.ds(j * page_len, page_len)
            copies.append(pltpu.make_async_copy(pool.at[table[j], value_slot], values.at[at], sems.at[1, j]))
        for c in copies:
            c.start()
        for c in copies:
            c.wait()

    scores = scores_of(queries[...], keys[...])
    at = lax.broadcasted_iota(jnp.int32, (1, scores.shape[1]), 1)
    scores = jnp.where(at < length, scores, -jnp.inf)
    top = jnp.max(scores, axis=1, keepdims=True)
    expo = jnp.exp(scores - top)
    top_out[...] = top
    total_out[...] = jnp.sum(expo, axis=1, keepdims=True)
    acc_out[...] = matmul(expo.astype(jnp.bfloat16), values[...])


def new_body(place, queries, own, first, second, acc, top_in, total_in, w_out, part_out, key, value):
    heads, rows, head_dim = queries.shape
    new_rows = own.shape[0]

    @pl.when(pl.program_id(0) == 0)
    def _():
        for at, source in enumerate((own, first, second)):
            for which, kept in enumerate((key, value)):

                @pl.when(place[which] == at)
                def _(source=source, kept=kept):
                    kept[...] = source[...]

    row_at = lax.broadcasted_iota(jnp.int32, (rows, new_rows), 0) + pl.program_id(0) * rows
    causal = lax.broadcasted_iota(jnp.int32, (rows, new_rows), 1) <= row_at
    sides = []
    for h in range(heads):
        scores = jnp.where(causal, scores_of(queries[h], key[...]), -jnp.inf)
        top_old = top_in[h]
        top = jnp.maximum(top_old, jnp.max(scores, axis=1, keepdims=True))
        expo = jnp.exp(scores - top)
        scale = jnp.exp(top_old - top)
        total = total_in[h] * scale + jnp.sum(expo, axis=1, keepdims=True)
        mix = acc[h] * scale + matmul(expo.astype(jnp.bfloat16), value[...])
        sides.append((mix / total).astype(jnp.bfloat16))
    attn = jnp.concatenate(sides, axis=1)
    part_out[...] = matmul(attn, w_out[...]).astype(jnp.bfloat16)


def base_body(place, hidden, in_gain, left, right, laurel_gain, base_out):
    tokens = hidden[...].astype(jnp.float32)
    normed = (rms_scale(tokens) * in_gain[...]).astype(jnp.bfloat16)
    low = matmul(normed, left[...]).astype(jnp.bfloat16)
    laurel = normed.astype(jnp.float32) + rms_scale(matmul(low, right[...])) * laurel_gain[...]
    base_out[...] = tokens + laurel


def tail_body(base, proj, post_gain, layer_input, w_plgate, w_plproj, pl_gain, out):
    state = (base[...] + rms_scale(proj[...].astype(jnp.float32)) * post_gain[...]) * 2.0 ** (-0.5)
    gate = jax.nn.gelu(matmul(state.astype(jnp.bfloat16), w_plgate[...]), approximate=True)
    gated = (gate * layer_input[...].astype(jnp.float32)).astype(jnp.bfloat16)
    out[...] = (state + rms_scale(matmul(gated, w_plproj[...])) * pl_gain[...]).astype(jnp.bfloat16)


def line_scatter(part, here, n, rows):
    def share(at):
        start = jnp.clip(at, 0, n - 1) * rows
        return lax.dynamic_slice_in_dim(part, start, rows, 0).astype(jnp.float32)

    up = jnp.zeros((), jnp.float32)
    down = jnp.zeros((), jnp.float32)
    for k in range(n - 1):
        send_up = (share(n - 1 - k + here) + up).astype(jnp.bfloat16)
        send_down = (share(k + here - n + 1) + down).astype(jnp.bfloat16)
        up = lax.ppermute(send_up, "head", [(z, z + 1) for z in range(k + 1)])
        down = lax.ppermute(send_down, "head", [(n - 1 - z, n - 2 - z) for z in range(k + 1)])
        up, down = up.astype(jnp.float32), down.astype(jnp.float32)
    return (share(here) + up + down).astype(jnp.bfloat16)


def on_device(
    hidden_in,
    layer_input,
    in_gain,
    w_query,
    w_keyval,
    q_gain,
    k_gain,
    w_out,
    post_gain,
    laurel_left,
    laurel_right,
    laurel_gain,
    w_plgate,
    w_plproj,
    pl_gain,
    kv_pool,
    page_table,
    prefix_len,
    decode_owner,
):
    new_rows, width = hidden_in.shape
    head_dim = kv_pool.shape[3]
    page_len = kv_pool.shape[2]
    n_pages = page_table.shape[1]
    kv_heads = kv_pool.shape[1] // 2
    local_heads = w_query.shape[1] // head_dim
    prefix_max = n_pages * page_len
    total_len = prefix_max + new_rows
    blocks = lax.axis_size("blk")
    block_span = total_len // blocks
    head_idx = lax.axis_index("head").astype(jnp.int32)
    kv_of = head_idx * local_heads // (QH // kv_heads)
    length = prefix_len[0]
    table = page_table[0]
    bf16, f32 = jnp.bfloat16, jnp.float32
    in_hbm = pl.BlockSpec(memory_space=pl.ANY)
    half_dim = head_dim // 2
    row = lambda v: v.reshape(1, -1)

    positions = length + jnp.arange(new_rows, dtype=jnp.int32)
    frequency = rope_base ** (-jnp.arange(half_dim, dtype=jnp.float32) / half_dim)
    angles = positions.astype(jnp.float32)[:, None] * frequency[None, :]
    cosine, sine = jnp.cos(angles), jnp.sin(angles)

    tile = new_rows // 2
    rows_of = lambda cols: pl.BlockSpec((tile, cols), lambda i, *_: (i, 0))
    queries, fresh = call(
        project_body,
        (
            jax.ShapeDtypeStruct((local_heads, new_rows, head_dim), bf16),
            jax.ShapeDtypeStruct((new_rows, head_dim), bf16),
        ),
        (new_rows // tile,),
        [
            rows_of(width),
            whole((1, width)),
            whole(w_query.shape),
            whole(w_keyval.shape),
            whole((1, head_dim)),
            whole((1, head_dim)),
            rows_of(half_dim),
            rows_of(half_dim),
        ],
        (
            pl.BlockSpec((local_heads, tile, head_dim), lambda i, *_: (0, i, 0)),
            rows_of(head_dim),
        ),
        [(head_idx < kv_heads).astype(jnp.int32).reshape(1)],
        [hidden_in, row(in_gain), w_query, w_keyval, row(q_gain), row(k_gain), cosine, sine],
        2 * new_rows * width * (local_heads + 1) * head_dim,
        8 << 20,
    )

    first = lax.ppermute(fresh, "head", [(0, 1), (1, 2), (2, 0)])
    second = lax.ppermute(fresh, "head", [(1, 3), (2, 1), (3, 2)])
    key_from = jnp.where(head_idx == 0, 0, jnp.where(head_idx == 3, 2, 1))
    value_from = jnp.where(head_idx == 0, 1, jnp.where(head_idx == 3, 0, 2))

    full_seq = call(
        sequence_body,
        jax.ShapeDtypeStruct((total_len, head_dim), bf16),
        (1,),
        [whole((new_rows, head_dim)), in_hbm],
        whole((total_len, head_dim)),
        [table, jnp.stack([length, head_idx])],
        [fresh, kv_pool],
        1 << 20,
        4 << 20,
        [
            pltpu.VMEM((prefix_max, head_dim), bf16),
            pltpu.VMEM((total_len + 8, head_dim), f32),
            pltpu.SemaphoreType.DMA((n_pages,)),
        ],
    )
    place = jnp.stack([length, kv_of, kv_of + kv_heads])
    flat = local_heads * new_rows
    queries, full_seq = lax.optimization_barrier((queries, full_seq))
    spread = lax.all_to_all(
        full_seq.reshape(blocks, block_span, head_dim), "blk", split_axis=0, concat_axis=0, tiled=True
    )
    q_tile = flat // 4
    q_rows = lambda cols: pl.BlockSpec((q_tile, cols), lambda i, *_: (i, 0))
    acc, top, total = call(
        old_body,
        (
            jax.ShapeDtypeStruct((flat, head_dim), f32),
            jax.ShapeDtypeStruct((flat, 1), f32),
            jax.ShapeDtypeStruct((flat, 1), f32),
        ),
        (flat // q_tile,),
        [q_rows(head_dim), in_hbm],
        (q_rows(head_dim), q_rows(1), q_rows(1)),
        [table, place],
        [queries.reshape(flat, head_dim), kv_pool],
        10 << 30,
        8 << 20,
        [
            pltpu.VMEM((prefix_max, head_dim), bf16),
            pltpu.VMEM((prefix_max, head_dim), bf16),
            pltpu.SemaphoreType.DMA((2, n_pages)),
        ],
    )

    heads_of = lambda cols: pl.BlockSpec((local_heads, tile, cols), lambda i, *_: (0, i, 0))
    part = call(
        new_body,
        jax.ShapeDtypeStruct((new_rows, width), bf16),
        (new_rows // tile,),
        [
            heads_of(head_dim),
            whole((new_rows, head_dim)),
            whole((new_rows, head_dim)),
            whole((new_rows, head_dim)),
            heads_of(head_dim),
            heads_of(1),
            heads_of(1),
            whole(w_out.shape),
        ],
        rows_of(width),
        [jnp.stack([key_from, value_from]).astype(jnp.int32)],
        [
            queries,
            fresh,
            first,
            second,
            acc.reshape(local_heads, new_rows, head_dim),
            top.reshape(local_heads, new_rows, 1),
            total.reshape(local_heads, new_rows, 1),
            w_out,
        ],
        6 << 30,
        8 << 20,
        [pltpu.VMEM((new_rows, head_dim), bf16), pltpu.VMEM((new_rows, head_dim), bf16)],
    )
    part, spread = lax.optimization_barrier((part, spread))
    quarter = new_rows // lax.axis_size("head")
    proj_rows = line_scatter(part, head_idx, lax.axis_size("head"), quarter)

    rank = laurel_left.shape[1]
    gate_dim = w_plgate.shape[1]
    base = call(
        base_body,
        jax.ShapeDtypeStruct((quarter, width), f32),
        (1,),
        [
            pl.BlockSpec((quarter, width), lambda i, p: (p[0], 0)),
            whole((1, width)),
            whole((width, rank)),
            whole((rank, width)),
            whole((1, width)),
        ],
        whole((quarter, width)),
        [head_idx.reshape(1)],
        [hidden_in, row(in_gain), laurel_left, laurel_right, row(laurel_gain)],
        1 << 28,
        4 << 20,
    )

    arranged = call(
        arrange_body,
        jax.ShapeDtypeStruct(spread.shape, bf16),
        (1,),
        [whole(spread.shape)],
        whole(spread.shape),
        [decode_owner],
        [spread],
        1 << 10,
        2 << 20,
    )
    owned = lax.all_to_all(arranged, "blk", split_axis=0, concat_axis=0, tiled=True)

    mixed = call(
        tail_body,
        jax.ShapeDtypeStruct((quarter, width), bf16),
        (1,),
        [
            whole((quarter, width)),
            whole((quarter, width)),
            whole((1, width)),
            whole((quarter, gate_dim)),
            whole(w_plgate.shape),
            whole(w_plproj.shape),
            whole((1, width)),
        ],
        whole((quarter, width)),
        [],
        [base, proj_rows, row(post_gain), layer_input, w_plgate, w_plproj, row(pl_gain)],
        1 << 28,
        6 << 20,
    )
    return (mixed, owned.reshape(1, 1, total_len, head_dim))


def solution(mesh):
    in_specs = (
        P("blk", None),
        P(("blk", "head"), None),
        P(),
        P(None, "head"),
        P(None, "head"),
        P(),
        P(),
        P("head", None),
        P(),
        P(),
        P(),
        P(),
        P(),
        P(),
        P(),
        P("blk", None, None, None),
        P("blk", None),
        P("blk"),
        P(),
    )
    out_specs = (P(("blk", "head"), None), P("head", "blk", None, None))
    return jax.shard_map(
        on_device, mesh=mesh, in_specs=in_specs, out_specs=out_specs, check_vma=False
    )
```
